512 devices in a mesh: row: 16 (over y, core), col: 8 (over z), layer: 4 (over x).
Axes of the slice: x: 4, y: 8, z: 8, core: 2. Of those that a mesh axis runs over, the one named last changes fastest.
Arguments:
- matrix: bfloat16 [131072, 512], P(('row', 'col')), may hold values from -1.5 to 1.5
- pattern: int32 [2048, 8], replicated, may hold values from 0 to 2047, as said below
Outputs:
- sign_matrix: bfloat16 [131072, 512], P(('row', 'col'))
The draws below stay inside these ranges and needn't reach their ends.
Inputs may be any that keep to these rules, and one draw needn't show every extreme that they name: `pattern`: row i lists 8 different block columns; its first entry is i, and the others lie within 4 of i, counted cyclically modulo 2048.
All inputs are finite; a program needn't handle non-finite values.
Results may differ from the reference program's by a relative error of at most 0.0062.
Values may be sent and summed in bfloat16 or wider, within the bound.
A program may use at most 64 MiB of HBM per device.

```python
import math
import jax
import jax.numpy as jnp
from jax import lax

BS = 64
KB = 8
W = 4
ITERS = 2
NB = 2048
ORDER = 131072


def draw_matrix(key, part):
    key = jax.random.fold_in(key, 11)
    noise_key, magnitude_key, sign_key = jax.random.split(key, 3)
    spread = 0.5 / math.sqrt(KB * BS)
    noise_part = jax.random.truncated_normal(noise_key, -4.0, 4.0, (ORDER, KB * BS), jnp.float32) * spread
    magnitude = jnp.exp(jax.random.uniform(magnitude_key, (ORDER,), jnp.float32, math.log(0.25), math.log(0.9)))
    sign_flip = jnp.where(jax.random.bernoulli(sign_key, 0.5, (ORDER,)), 1.0, -1.0)
    row_number = jnp.arange(ORDER, dtype=jnp.int32)[:, None]
    column_number = jnp.arange(KB * BS, dtype=jnp.int32)[None, :]
    on_diagonal = (column_number < BS) & (column_number == row_number % BS)
    diagonal = jnp.where(on_diagonal, (magnitude * sign_flip)[:, None], 0.0)
    return (noise_part + diagonal).astype(jnp.bfloat16)


def draw_pattern(key, part):
    key = jax.random.fold_in(key, 23)
    row_keys = jax.random.split(key, NB)
    candidates = jnp.concatenate([jnp.arange(-W, 0, dtype=jnp.int32), jnp.arange(1, W + 1, dtype=jnp.int32)])

    def single_row(row_key, row_id):
        shuffled = jax.random.permutation(row_key, candidates)
        offsets = shuffled[:KB - 1]
        others = (row_id + offsets + NB) % NB
        return jnp.concatenate([row_id[None], others.astype(jnp.int32)])
    row_ids = jnp.arange(NB, dtype=jnp.int32)
    return jax.vmap(single_row)(row_keys, row_ids).astype(jnp.int32)


def setup_inputs(seed: int = 0) -> dict:
    seeds = jax.random.split(jax.random.key(seed), 3)
    return {
        "matrix": draw_matrix(jax.random.fold_in(seeds[2], 71), 0),
        "pattern": draw_pattern(jax.random.fold_in(seeds[2], 71), 0),
    }


def block_product(left, right, pattern):
    neighbour = jnp.take(pattern, pattern, axis=0)
    matches = neighbour[:, :, None, :] == pattern[:, None, :, None]
    present = jnp.any(matches, axis=3)
    slot_numbers = jnp.arange(KB, dtype=jnp.int32)
    picked_slot = jnp.sum(jnp.where(matches, slot_numbers, 0), axis=3).astype(jnp.int32)
    left_blocks = left.astype(jnp.float32).reshape(NB, BS, KB, BS)
    right_blocks = right.astype(jnp.float32).reshape(NB, BS, KB, BS).transpose(0, 2, 1, 3)

    def single_row(row_number):
        sources = pattern[row_number]
        chosen = right_blocks[sources[:, None], picked_slot[row_number]]
        chosen = jnp.where(present[row_number][:, :, None, None], chosen, jnp.zeros_like(chosen))
        return jnp.einsum("asb,szbc->azc", left_blocks[row_number], chosen, precision=lax.Precision.HIGHEST)

    row_results = lax.map(single_row, jnp.arange(NB, dtype=jnp.int32))
    return row_results.reshape(NB * BS, KB * BS)


def reference(matrix, pattern):
    row_number = jnp.arange(NB * BS, dtype=jnp.int32)[:, None]
    column_number = jnp.arange(KB * BS, dtype=jnp.int32)[None, :]
    identity = jnp.where((column_number < BS) & (column_number == row_number % BS), 1.0, 0.0).astype(jnp.float32)
    current = matrix
    for iteration in range(ITERS):
        squared = block_product(current, current, pattern)
        factor = (1.5 * identity - 0.5 * squared).astype(jnp.bfloat16)
        current = block_product(current, factor, pattern).astype(jnp.bfloat16)
    return current
```

```python
import jax
import jax.numpy as jnp
from jax import lax
from jax.experimental import pallas as pl
from jax.experimental.pallas import tpu as pltpu
from jax.sharding import PartitionSpec as P

BS = 64
KB = 8
W = 4
SB = W * BS
GROUP = 16
TILE = 128 // GROUP
BUF = 8 * 128
MESH = pl.DeviceIdType.MESH
F32 = jnp.float32
BF16 = jnp.bfloat16


def kernel(
    groups, cols, x_hbm, pat_hbm, out_hbm,
    loc, a_lo, a_hi, b_lo, b_hi, c_lo, c_hi, xd, f0, x1, f1, x2, out_v,
    pat_v, tab_v, tab_s, load_sem, pat_sem, tab_sem, out_sem, send_sem, recv_sem,
):
    row, col, layer = lax.axis_index("row"), lax.axis_index("col"), lax.axis_index("layer")
    me = row * cols + col
    before, after = lax.rem(me + groups - 1, groups), lax.rem(me + 1, groups)

    def device(group):
        return (group // cols, lax.rem(group, cols), layer)

    barrier = pltpu.get_barrier_semaphore()
    for group in (before, after):
        pl.semaphore_signal(barrier, inc=1, device_id=device(group), device_id_type=MESH)

    load = pltpu.make_async_copy(x_hbm, loc.at[:, 0 : KB * BS], load_sem)
    load.start()
    def tile_of(group):
        return pl.ds(pl.multiple_of((group // TILE) * 128, 128), 128)

    pats = [
        pltpu.make_async_copy(pat_hbm.at[:, tile_of(group)], pat_v.at[q], pat_sem.at[q])
        for q, group in enumerate((before, me, after))
    ]
    for copy in pats:
        copy.start()
    for copy in pats:
        copy.wait()

    lane = lax.broadcasted_iota(jnp.int32, (KB, 128), 1)
    slot = lax.broadcasted_iota(jnp.int32, (KB, 128), 0)
    a_of = lane & (W - 1)

    def slot_sum(v):
        for step in (1, 2, 4):
            v = v + pltpu.roll(v, step, 0)
        return v[0:1]

    for q, group in enumerate((before, me, after)):
        off = (pat_v[q] - ((group // TILE) * 128 + lane) + W) & (groups * GROUP - 1)
        for o in range(2 * W + 1):
            code = ((slot ^ (a_of + o)) & 1) * 4 + (slot >> 1) - 8
            tab_v[q, o : o + 1, :] = 8 + slot_sum(jnp.where(off == o, code, 0))
        tab_v[q, 9:10, :] = W * (2 * W + 1) - slot_sum(off)
        if q == 1:
            place = a_of + off
            tab_v[3, 0:KB, :] = ((place ^ slot) & 1) * 6 + (place >> 1)
    table = pltpu.make_async_copy(tab_v, tab_s, tab_sem)
    table.start()
    first_lane = [lax.rem(group, TILE) * GROUP for group in (before, me, after)]

    pl.semaphore_wait(barrier, 2)

    def send(index, src, dst, group):
        return pltpu.make_async_remote_copy(
            src_ref=src, dst_ref=dst, send_sem=send_sem.at[index], recv_sem=recv_sem.at[index],
            device_id=device(group), device_id_type=MESH,
        )

    wide = KB * BS
    copies = {
        ("a", 0): send(0, x_hbm.at[pl.ds(3 * SB, SB)], a_lo.at[:, 0:wide], after),
        ("a", 1): send(1, x_hbm.at[pl.ds(0, SB)], a_hi.at[:, 0:wide], before),
        ("b", 0): send(2, x_hbm.at[pl.ds(2 * SB, SB)], b_lo.at[:, 0:wide], after),
        ("b", 1): send(3, x_hbm.at[pl.ds(SB, SB)], b_hi.at[:, 0:wide], before),
        ("c", 0): send(4, xd.at[pl.ds(3 * SB, SB), 2 * SB : 3 * SB], c_lo, after),
        ("c", 1): send(5, xd.at[pl.ds(4 * SB, SB), 0:SB], c_hi, before),
    }
    for key in (("a", 0), ("a", 1), ("b", 0), ("b", 1)):
        copies[key].start()

    def swap(v):
        return jnp.concatenate([v[:, BS:], v[:, :BS]], axis=1)

    left_half = lax.broadcasted_iota(jnp.int32, (1, 128), 1) < BS

    def pick(planes, first, second):
        number = jnp.where(left_half, first, second).astype(F32).astype(BF16)
        number = jnp.broadcast_to(number, (BS, 128))
        value = jnp.zeros((BS, 128), BF16)
        for index, plane in planes.items():
            value = jnp.where(number == jnp.array(index, BF16), plane, value)
        return value

    def densify(src, src_base, dst_base, q, first):
        rows = pl.ds(src_base, SB)
        for d in range(4):
            src[rows, 512 + 128 * d : 640 + 128 * d] = swap(src[rows, 128 * d : 128 * d + 128])
        for a in range(W):
            rows = pl.ds(src_base + a * BS, BS)
            planes = {d: src[rows, 128 * d : 128 * d + 128] for d in range(8)}
            for d in range(6):
                number = [
                    tab_s[q, o, first_lane[q] + first + a] if 0 <= o <= 2 * W else 8 for o in (2 * d - a, 2 * d + 1 - a)
                ]
                if all(isinstance(n, int) for n in number):
                    value = jnp.zeros((BS, 128), BF16)
                else:
                    value = pick(planes, *number)
                xd[pl.ds(dst_base + a * BS, BS), 128 * d : 128 * d + 128] = value

    load.wait()
    table.wait()

    def local_rows(index, carry):
        densify(loc, index * SB, (index + 2) * SB, 1, index * W)
        return carry

    lax.fori_loop(0, GROUP // W, local_rows, 0)
    copies[("c", 0)].start()
    copies[("c", 1)].start()

    block_lane = lax.broadcasted_iota(jnp.int32, (1, SB), 1) >> 6
    eye = jnp.where(
        lax.broadcasted_iota(jnp.int32, (SB, SB), 0) == lax.broadcasted_iota(jnp.int32, (SB, SB), 1), 1.5, 0.0
    ).astype(F32)

    def block(ref, i, j):
        return ref[(i + 2) * SB : (i + 3) * SB, (j - i + 1) * SB : (j - i + 2) * SB]

    def product(left, right, i, j):
        ks = [k for k in (i - 1, i, i + 1) if abs(k - j) <= 1]
        lo = ks[0] - i + 1
        lhs = left[(i + 2) * SB : (i + 3) * SB, lo * SB : (lo + len(ks)) * SB]
        rhs = []
        for k in ks:
            if right is xd and k == -3:
                rhs.append(c_lo[...])
            elif right is xd and k == 6:
                rhs.append(c_hi[...])
            else:
                rhs.append(block(right, k, j))
        return jnp.dot(lhs, jnp.concatenate(rhs, axis=0), preferred_element_type=F32)

    def masks(i, j):
        out = []
        for a in range(W):
            r = i * W + a
            q, r = (0, r + GROUP) if r < 0 else ((2, r - GROUP) if r >= GROUP else (1, r))
            o = block_lane + ((j - i + 1) * W - a)
            keep = (o != tab_s[q, 9, first_lane[q] + r]) & (o >= 0) & (o <= 2 * W)
            out.append(jnp.where(keep, 1.0, 0.0).astype(F32))
        return out

    def step(dst, left, right, i, j, factor):
        value = product(left, right, i, j)
        keep = masks(i, j)
        pieces = []
        for a in range(W):
            piece = value[a * BS : (a + 1) * BS]
            if factor:
                piece = piece * (keep[a] * -0.5)
                if i == j:
                    piece = piece + eye[a * BS : (a + 1) * BS]
            else:
                piece = piece * keep[a]
            pieces.append(piece.astype(BF16))
        if dst is x2:
            for a in range(W):
                for h in range(2):
                    d = (j - i + 1) * 2 + h
                    part = pieces[a][:, h * 128 : (h + 1) * 128]
                    rows = slice(i * SB + a * BS, i * SB + (a + 1) * BS)
                    x2[rows, d * 128 : d * 128 + 128] = part
                    x2[rows, (d + 6) * 128 : (d + 6) * 128 + 128] = swap(part)
        else:
            for a in range(W):
                top = (i + 2) * SB + a * BS
                dst[top : top + BS, (j - i + 1) * SB : (j - i + 2) * SB] = pieces[a]

    def level(dst, left, right, pairs, factor):
        for i, j in pairs:
            step(dst, left, right, i, j, factor)
            step(dst, left, right, 3 - i, 3 - j, factor)

    def stage(f0_pairs, x1_pairs, f1_pairs, x2_pairs):
        level(f0, xd, xd, f0_pairs, True)
        level(x1, xd, f0, x1_pairs, False)
        level(f1, x1, x1, f1_pairs, True)
        level(x2, x1, f1, x2_pairs, False)

    outs = []

    def finish(i):
        for a in range(W):
            r = i * W + a
            rows = slice(r * BS, (r + 1) * BS)
            chunks = range(a // 2, a // 2 + W + 1)
            planes = {d: x2[rows, 128 * d : 128 * d + 128] for base in (0, 6) for d in (base + c for c in chunks)}
            for d in range(4):
                number = [tab_s[3, s, first_lane[1] + r] for s in (2 * d, 2 * d + 1)]
                out_v[rows, 128 * d : 128 * d + 128] = pick(planes, *number)
        copy = pltpu.make_async_copy(out_v.at[pl.ds(i * SB, SB)], out_hbm.at[pl.ds(i * SB, SB)], out_sem.at[i])
        copy.start()
        outs.append(copy)

    stage([(0, 1), (1, 0), (1, 1), (1, 2)], [(0, 1), (1, 1), (1, 2)], [(1, 2)], [])

    copies[("a", 0)].wait_recv()
    densify(a_lo, 0, SB, 0, 12)
    copies[("a", 1)].wait_recv()
    densify(a_hi, 0, 6 * SB, 2, 0)
    stage([(0, 0), (0, -1), (-1, 0)], [(0, 0), (1, 0), (-1, 0)], [(0, 1), (1, 0), (1, 1)], [(0, 1), (1, 1), (1, 2)])

    copies[("b", 0)].wait_recv()
    densify(b_lo, 0, 0, 0, 8)
    copies[("b", 1)].wait_recv()
    densify(b_hi, 0, 7 * SB, 2, 4)
    stage([(-1, -1), (-1, -2), (-2, -1)], [(0, -1), (-1, -1), (-2, -1)], [(0, 0), (0, -1), (-1, 0)], [(0, 0), (1, 0)])
    finish(1)
    finish(2)

    copies[("c", 0)].wait_recv()
    copies[("c", 1)].wait_recv()
    stage([(-2, -2)], [(-1, -2)], [(-1, -1)], [(0, -1)])
    finish(0)
    finish(3)

    for copy in outs:
        copy.wait()
    for copy in copies.values():
        copy.wait_send()


def solution(mesh):
    groups = mesh.shape["row"] * mesh.shape["col"]
    cols = mesh.shape["col"]

    def on_device(matrix, pattern):
        rows = GROUP * BS

        def body(*refs):
            kernel(groups, cols, *refs)

        any_space = pl.BlockSpec(memory_space=pl.ANY)
        return pl.pallas_call(
            body,
            out_shape=jax.ShapeDtypeStruct((rows, KB * BS), BF16),
            in_specs=[any_space, any_space],
            out_specs=any_space,
            scratch_shapes=[
                pltpu.VMEM((rows, BUF), BF16),
                pltpu.VMEM((SB, BUF), BF16),
                pltpu.VMEM((SB, BUF), BF16),
                pltpu.VMEM((SB, BUF), BF16),
                pltpu.VMEM((SB, BUF), BF16),
                pltpu.VMEM((SB, SB), BF16),
                pltpu.VMEM((SB, SB), BF16),
                pltpu.VMEM((8 * SB, 3 * SB), BF16),
                pltpu.VMEM((8 * SB, 3 * SB), BF16),
                pltpu.VMEM((8 * SB, 3 * SB), BF16),
                pltpu.VMEM((8 * SB, 3 * SB), BF16),
                pltpu.VMEM((rows, 12 * 128), BF16),
                pltpu.VMEM((rows, KB * BS), BF16),
                pltpu.VMEM((3, KB, 128), jnp.int32),
                pltpu.VMEM((4, 16, 128), jnp.int32),
                pltpu.SMEM((4, 16, 128), jnp.int32),
                pltpu.SemaphoreType.DMA,
                pltpu.SemaphoreType.DMA((3,)),
                pltpu.SemaphoreType.DMA,
                pltpu.SemaphoreType.DMA((4,)),
                pltpu.SemaphoreType.DMA((6,)),
                pltpu.SemaphoreType.DMA((6,)),
            ],
            compiler_params=pltpu.CompilerParams(
                collective_id=0, has_side_effects=True, vmem_limit_bytes=62 * 1024 * 1024
            ),
            cost_estimate=pl.CostEstimate(flops=164 * 2 * SB**3, bytes_accessed=8 << 20, transcendentals=0),
        )(matrix, pattern.T)

    return jax.shard_map(
        on_device,
        mesh=mesh,
        in_specs=(P(("row", "col"), None), P()),
        out_specs=P(("row", "col"), None),
        check_vma=False,
    )
```

```python
import jax
import jax.numpy as jnp
from jax import lax
from jax.experimental import pallas as pl
from jax.experimental.pallas import tpu as pltpu
from jax.sharding import PartitionSpec as P

BS = 64
KB = 8
W = 4
SB = W * BS
GROUP = 16
TILE = 128 // GROUP
BUF = 8 * 128
MESH = pl.DeviceIdType.MESH
F32 = jnp.float32
BF16 = jnp.bfloat16


def kernel(
    groups, cols, x_hbm, pat_hbm, out_hbm,
    loc, a_lo, a_hi, xd, f0, x1, f1, x2, out_v,
    pat_v, tab_v, tab_s, load_sem, pat_sem, tab_sem, out_sem, z_send, z_recv, x_send, x_recv, late,
):
    row, col, layer = lax.axis_index("row"), lax.axis_index("col"), lax.axis_index("layer")
    me = row * cols + col
    before, after = lax.rem(me + groups - 1, groups), lax.rem(me + 1, groups)

    first, last = col == 0, col == cols - 1
    part = lax.rem(layer, 2)
    partner = (row, col, layer + 1 - 2 * part)

    def device(group):
        return (group // cols, lax.rem(group, cols), layer)

    barrier = pltpu.get_barrier_semaphore()
    pl.semaphore_signal(barrier, inc=1, device_id=device(before), device_id_type=MESH)
    pl.semaphore_signal(barrier, inc=1, device_id=partner, device_id_type=MESH)

    @pl.when(jnp.logical_not(last))
    def _():
        pl.semaphore_signal(barrier, inc=1, device_id=device(after), device_id_type=MESH)

    load = pltpu.make_async_copy(x_hbm, loc.at[:, 0 : KB * BS], load_sem)
    load.start()
    def tile_of(group):
        return pl.ds(pl.multiple_of((group // TILE) * 128, 128), 128)

    pats = [
        pltpu.make_async_copy(pat_hbm.at[:, tile_of(group)], pat_v.at[q], pat_sem.at[q])
        for q, group in enumerate((before, me, after))
    ]
    for copy in pats:
        copy.start()
    for copy in pats:
        copy.wait()

    lane = lax.broadcasted_iota(jnp.int32, (KB, 128), 1)
    slot = lax.broadcasted_iota(jnp.int32, (KB, 128), 0)
    a_of = lane & (W - 1)

    def slot_sum(v):
        for step in (1, 2, 4):
            v = v + pltpu.roll(v, step, 0)
        return v[0:1]

    for q, group in enumerate((before, me, after)):
        off = (pat_v[q] - ((group // TILE) * 128 + lane) + W) & (groups * GROUP - 1)
        for o in range(2 * W + 1):
            code = ((slot ^ (a_of + o)) & 1) * 4 + (slot >> 1) - 8
            tab_v[q, o : o + 1, :] = 8 + slot_sum(jnp.where(off == o, code, 0))
        tab_v[q, 9:10, :] = W * (2 * W + 1) - slot_sum(off)
        if q == 1:
            place = a_of + off
            tab_v[3, 0:KB, :] = ((place ^ slot) & 1) * 6 + (place >> 1)
    table = pltpu.make_async_copy(tab_v, tab_s, tab_sem)
    table.start()
    first_lane = [lax.rem(group, TILE) * GROUP for group in (before, me, after)]

    @pl.when(first)
    def _():
        pl.semaphore_wait(barrier, 2)

    @pl.when(jnp.logical_not(first))
    def _():
        pl.semaphore_wait(barrier, 3)

    @pl.when(last)
    def _():
        pl.semaphore_signal(late, inc=1, device_id=device(after), device_id_type=MESH)

    def piece(side, index, half, source):
        def lanes(base, count, step):
            return pl.ds(pl.multiple_of(base + step * half, 128), count)

        if index < 2:
            rows = pl.ds((3 * SB if source and side == 0 else 0) + 128 * half + 64 * index, 64)
            return x_hbm.at[rows] if source else (a_lo, a_hi)[side].at[rows, 0 : KB * BS]
        if index < 5:
            base = ((4, 3) if source else (0, 7))[side] * SB
            left = (2 * SB, 0)[side]
            if index == 2:
                return xd.at[pl.ds(base + 128 * half, 128), SB : 2 * SB]
            if index == 3:
                return xd.at[pl.ds(base + 128 * half, 128), lanes(left, 128, 128)]
            return xd.at[pl.ds(base + (128, 0)[side] + 64 * half, 64), pl.ds(left + (0, 128)[side], 128)]
        base = ((5, 2) if source else (1, 6))[side] * SB
        left = (0, 2 * SB)[side]
        if index == 5:
            return x1.at[pl.ds(base + 128 * half, 128), lanes(left, 128, 128)]
        return x1.at[pl.ds(base + (0, 128)[side] + 64 * half, 64), pl.ds(left + (128, 0)[side], 128)]

    def over_z(side, index):
        return pltpu.make_async_remote_copy(
            src_ref=piece(side, index, part, True), dst_ref=piece(side, index, part, False),
            send_sem=z_send.at[side, index], recv_sem=z_recv.at[side, index],
            device_id=device((after, before)[side]), device_id_type=MESH,
        )

    def over_x(side, index, half):
        ref = piece(side, index, half, False)
        return pltpu.make_async_remote_copy(
            src_ref=ref, dst_ref=ref,
            send_sem=x_send.at[side, index], recv_sem=x_recv.at[side, index],
            device_id=partner, device_id_type=MESH,
        )

    def send(indices):
        for index in indices:
            over_z(0, index).start()

        @pl.when(jnp.logical_not(first))
        def _():
            for index in indices:
                over_z(1, index).start()

    def forward(side, indices):
        for index in indices:
            over_z(side, index).wait_recv()
            over_x(side, index, part).start()

    def arrive(side, indices):
        for index in indices:
            over_x(side, index, 1 - part).wait_recv()

    SLOTS, NEXT, TRIANGLE = (0, 1), (2, 3, 4), (5, 6)
    send(SLOTS)

    def swap(v):
        return jnp.concatenate([v[:, BS:], v[:, :BS]], axis=1)

    left_half = lax.broadcasted_iota(jnp.int32, (1, 128), 1) < BS

    def pick(planes, first, second):
        number = jnp.where(left_half, first, second).astype(F32).astype(BF16)
        number = jnp.broadcast_to(number, (BS, 128))
        value = jnp.zeros((BS, 128), BF16)
        for index, plane in planes.items():
            value = jnp.where(number == jnp.array(index, BF16), plane, value)
        return value

    def densify(src, src_base, dst_base, q, first):
        rows = pl.ds(src_base, SB)
        for d in range(4):
            src[rows, 512 + 128 * d : 640 + 128 * d] = swap(src[rows, 128 * d : 128 * d + 128])
        for a in range(W):
            rows = pl.ds(src_base + a * BS, BS)
            planes = {d: src[rows, 128 * d : 128 * d + 128] for d in range(8)}
            for d in range(6):
                number = [
                    tab_s[q, o, first_lane[q] + first + a] if 0 <= o <= 2 * W else 8 for o in (2 * d - a, 2 * d + 1 - a)
                ]
                if all(isinstance(n, int) for n in number):
                    value = jnp.zeros((BS, 128), BF16)
                else:
                    value = pick(planes, *number)
                xd[pl.ds(dst_base + a * BS, BS), 128 * d : 128 * d + 128] = value

    load.wait()
    table.wait()

    def local_rows(index, carry):
        densify(loc, index * SB, (index + 2) * SB, 1, index * W)
        return carry

    lax.fori_loop(0, GROUP // W, local_rows, 0)
    send(NEXT)
    blank = jnp.zeros((128, 128), BF16)
    xd[0:128, 640:768] = blank
    xd[7 * SB + 128 : 8 * SB, 0:128] = blank
    x1[SB + 128 : 2 * SB, 0:128] = blank
    x1[6 * SB : 6 * SB + 128, 640:768] = blank

    block_lane = lax.broadcasted_iota(jnp.int32, (1, SB), 1) >> 6
    eye = jnp.where(
        lax.broadcasted_iota(jnp.int32, (SB, SB), 0) == lax.broadcasted_iota(jnp.int32, (SB, SB), 1), 1.5, 0.0
    ).astype(F32)

    def block(ref, i, j):
        return ref[(i + 2) * SB : (i + 3) * SB, (j - i + 1) * SB : (j - i + 2) * SB]

    def product(left, right, i, j):
        ks = [k for k in (i - 1, i, i + 1) if abs(k - j) <= 1]
        lo = ks[0] - i + 1
        lhs = left[(i + 2) * SB : (i + 3) * SB, lo * SB : (lo + len(ks)) * SB]
        rhs = []
        for k in ks:
            rhs.append(block(right, k, j))
        return jnp.dot(lhs, jnp.concatenate(rhs, axis=0), preferred_element_type=F32)

    def masks(i, j):
        out = []
        for a in range(W):
            r = i * W + a
            q, r = (0, r + GROUP) if r < 0 else ((2, r - GROUP) if r >= GROUP else (1, r))
            o = block_lane + ((j - i + 1) * W - a)
            keep = (o != tab_s[q, 9, first_lane[q] + r]) & (o >= 0) & (o <= 2 * W)
            out.append(jnp.where(keep, 1.0, 0.0).astype(F32))
        return out

    def step(dst, left, right, i, j, factor):
        value = product(left, right, i, j)
        keep = masks(i, j)
        pieces = []
        for a in range(W):
            piece = value[a * BS : (a + 1) * BS]
            if factor:
                piece = piece * (keep[a] * -0.5)
                if i == j:
                    piece = piece + eye[a * BS : (a + 1) * BS]
            else:
                piece = piece * keep[a]
            pieces.append(piece.astype(BF16))
        if dst is x2:
            for a in range(W):
                for h in range(2):
                    d = (j - i + 1) * 2 + h
                    part = pieces[a][:, h * 128 : (h + 1) * 128]
                    rows = slice(i * SB + a * BS, i * SB + (a + 1) * BS)
                    x2[rows, d * 128 : d * 128 + 128] = part
                    x2[rows, (d + 6) * 128 : (d + 6) * 128 + 128] = swap(part)
        else:
            for a in range(W):
                top = (i + 2) * SB + a * BS
                dst[top : top + BS, (j - i + 1) * SB : (j - i + 2) * SB] = pieces[a]

    def level(sides, dst, left, right, pairs, factor):
        for i, j in pairs:
            for side in sides:
                step(dst, left, right, *((i, j) if side == 0 else (3 - i, 3 - j)), factor)

    def level_f0(sides, pairs):
        level(sides, f0, xd, xd, pairs, True)

    def level_x1(sides, pairs):
        level(sides, x1, xd, f0, pairs, False)

    def level_f1(sides, pairs):
        level(sides, f1, x1, x1, pairs, True)

    def level_x2(sides, pairs):
        level(sides, x2, x1, f1, pairs, False)

    outs = []

    def finish(i):
        for a in range(W):
            r = i * W + a
            rows = slice(r * BS, (r + 1) * BS)
            chunks = range(a // 2, a // 2 + W + 1)
            planes = {d: x2[rows, 128 * d : 128 * d + 128] for base in (0, 6) for d in (base + c for c in chunks)}
            for d in range(4):
                number = [tab_s[3, s, first_lane[1] + r] for s in (2 * d, 2 * d + 1)]
                out_v[rows, 128 * d : 128 * d + 128] = pick(planes, *number)
        copy = pltpu.make_async_copy(out_v.at[pl.ds(i * SB, SB)], out_hbm.at[pl.ds(i * SB, SB)], out_sem.at[i])
        copy.start()
        outs.append(copy)

    both = (0, 1)
    level_f0(both, [(0, 1), (1, 0), (1, 1), (1, 2)])
    level_x1(both, [(0, 1), (1, 1), (1, 2)])
    send(TRIANGLE)
    level_f1(both, [(1, 2)])

    def near(side):
        arrive(side, SLOTS)
        densify((a_lo, a_hi)[side], 0, (SB, 6 * SB)[side], (0, 2)[side], (12, 0)[side])
        level_f0((side,), [(0, 0), (0, -1), (-1, 0)])
        level_x1((side,), [(0, 0), (1, 0), (-1, 0)])
        level_f1((side,), [(0, 1), (1, 0), (1, 1)])
        level_x2((side,), [(0, 1), (1, 1)])

    def farther(side):
        arrive(side, NEXT)
        level_f0((side,), [(-1, -1), (-2, -1)])
        level_x1((side,), [(0, -1), (-1, -1), (-2, -1)])
        level_f1((side,), [(0, 0), (0, -1), (-1, 0)])
        level_x2((side,), [(0, 0), (1, 0)])

    def farthest(side):
        arrive(side, TRIANGLE)
        level_f1((side,), [(-1, -1)])
        level_x2((side,), [(0, -1)])

    forward(1, SLOTS)
    near(1)
    forward(1, NEXT)
    forward(1, TRIANGLE)

    @pl.when(first)
    def _():
        pl.semaphore_wait(late, 1)
        for index in SLOTS + NEXT + TRIANGLE:
            over_z(1, index).start()

    forward(0, SLOTS)
    farther(1)
    farthest(1)
    finish(3)
    forward(0, NEXT)
    near(0)
    level_x2(both, [(1, 2)])
    finish(2)
    forward(0, TRIANGLE)
    farther(0)
    finish(1)
    farthest(0)
    finish(0)

    for copy in outs:
        copy.wait()
    for side in both:
        for index in SLOTS + NEXT + TRIANGLE:
            over_z(side, index).wait_send()
            over_x(side, index, part).wait_send()


def solution(mesh):
    groups = mesh.shape["row"] * mesh.shape["col"]
    cols = mesh.shape["col"]

    def on_device(matrix, pattern):
        rows = GROUP * BS

        def body(*refs):
            kernel(groups, cols, *refs)

        any_space = pl.BlockSpec(memory_space=pl.ANY)
        return pl.pallas_call(
            body,
            out_shape=jax.ShapeDtypeStruct((rows, KB * BS), BF16),
            in_specs=[any_space, any_space],
            out_specs=any_space,
            scratch_shapes=[
                pltpu.VMEM((rows, BUF), BF16),
                pltpu.VMEM((SB, BUF), BF16),
                pltpu.VMEM((SB, BUF), BF16),
                pltpu.VMEM((8 * SB, 3 * SB), BF16),
                pltpu.VMEM((8 * SB, 3 * SB), BF16),
                pltpu.VMEM((8 * SB, 3 * SB), BF16),
                pltpu.VMEM((8 * SB, 3 * SB), BF16),
                pltpu.VMEM((rows, 12 * 128), BF16),
                pltpu.VMEM((rows, KB * BS), BF16),
                pltpu.VMEM((3, KB, 128), jnp.int32),
                pltpu.VMEM((4, 16, 128), jnp.int32),
                pltpu.SMEM((4, 16, 128), jnp.int32),
                pltpu.SemaphoreType.DMA,
                pltpu.SemaphoreType.DMA((3,)),
                pltpu.SemaphoreType.DMA,
                pltpu.SemaphoreType.DMA((4,)),
                pltpu.SemaphoreType.DMA((2, 7)),
                pltpu.SemaphoreType.DMA((2, 7)),
                pltpu.SemaphoreType.DMA((2, 7)),
                pltpu.SemaphoreType.DMA((2, 7)),
                pltpu.SemaphoreType.REGULAR,
            ],
            compiler_params=pltpu.CompilerParams(
                collective_id=0, has_side_effects=True, vmem_limit_bytes=62 * 1024 * 1024
            ),
            cost_estimate=pl.CostEstimate(flops=150 * 2 * SB**3, bytes_accessed=8 << 20, transcendentals=0),
        )(matrix, pattern.T)

    return jax.shard_map(
        on_device,
        mesh=mesh,
        in_specs=(P(("row", "col"), None), P()),
        out_specs=P(("row", "col"), None),
        check_vma=False,
    )
```

```python
import jax
import jax.numpy as jnp
from jax import lax
from jax.experimental import pallas as pl
from jax.experimental.pallas import tpu as pltpu
from jax.sharding import PartitionSpec as P

BS = 64
KB = 8
W = 4
SB = W * BS
GROUP = 16
TILE = 128 // GROUP
BUF = 8 * 128
MESH = pl.DeviceIdType.MESH
F32 = jnp.float32
BF16 = jnp.bfloat16


def kernel(
    groups, cols, x_hbm, pat_hbm, out_hbm,
    loc, a_lo, a_hi, xd, f0, x1, f1, x2, out_v,
    pat_v, tab_v, tab_s, load_sem, pat_sem, tab_sem, out_sem, z_send, z_recv, x_send, late, late_x,
):
    row, col, layer = lax.axis_index("row"), lax.axis_index("col"), lax.axis_index("layer")
    me = row * cols + col
    before, after = lax.rem(me + groups - 1, groups), lax.rem(me + 1, groups)

    first, last = col == 0, col == cols - 1
    part = lax.rem(layer, 2)
    partner = (row, col, layer + 1 - 2 * part)

    def device(group):
        return (group // cols, lax.rem(group, cols), layer)

    edge = jnp.logical_or(first, last)
    edge_even, edge_odd = jnp.logical_and(edge, part == 0), jnp.logical_and(edge, part == 1)
    barrier = pltpu.get_barrier_semaphore()
    pl.semaphore_signal(barrier, inc=1, device_id=device(before), device_id_type=MESH)

    @pl.when(edge_even)
    def _():
        pl.semaphore_signal(barrier, inc=1, device_id=partner, device_id_type=MESH)

    @pl.when(jnp.logical_not(last))
    def _():
        pl.semaphore_signal(barrier, inc=1, device_id=device(after), device_id_type=MESH)

    load = pltpu.make_async_copy(x_hbm, loc.at[:, 0 : KB * BS], load_sem)
    load.start()
    def tile_of(group):
        return pl.ds(pl.multiple_of((group // TILE) * 128, 128), 128)

    pats = [
        pltpu.make_async_copy(pat_hbm.at[:, tile_of(group)], pat_v.at[q], pat_sem.at[q])
        for q, group in enumerate((before, me, after))
    ]
    for copy in pats:
        copy.start()
    pl.semaphore_wait(barrier, 2 - jnp.where(first, 1, 0) + jnp.where(edge_odd, 1, 0))

    @pl.when(edge_odd)
    def _():
        pl.semaphore_signal(late_x, inc=1, device_id=partner, device_id_type=MESH)

    @pl.when(last)
    def _():
        pl.semaphore_signal(late, inc=1, device_id=device(after), device_id_type=MESH)

    def piece(side, index, half, source):
        def lanes(base, count, step):
            return pl.ds(pl.multiple_of(base + step * half, 128), count)

        if index < 2:
            rows = pl.ds((3 * SB if source and side == 0 else 0) + 128 * half + 64 * index, 64)
            return x_hbm.at[rows] if source else (a_lo, a_hi)[side].at[rows, 0 : KB * BS]
        if index < 5:
            base = ((4, 3) if source else (0, 7))[side] * SB
            left = (2 * SB, 0)[side]
            if index == 2:
                return xd.at[pl.ds(base + 128 * half, 128), SB : 2 * SB]
            if index == 3:
                return xd.at[pl.ds(base + 128 * half, 128), lanes(left, 128, 128)]
            return xd.at[pl.ds(base + (128, 0)[side] + 64 * half, 64), pl.ds(left + (0, 128)[side], 128)]
        base = ((5, 2) if source else (1, 6))[side] * SB
        left = (0, 2 * SB)[side]
        if index == 5:
            return x1.at[pl.ds(base + 128 * half, 128), lanes(left, 128, 128)]
        return x1.at[pl.ds(base + (0, 128)[side] + 64 * half, 64), pl.ds(left + (128, 0)[side], 128)]

    def over_z(side, index, half):
        mine = jnp.where(half == part, 0, 1)
        return pltpu.make_async_remote_copy(
            src_ref=piece(side, index, half, True), dst_ref=piece(side, index, half, False),
            send_sem=z_send.at[side, index, mine], recv_sem=z_recv.at[side, index, mine],
            device_id=device((after, before)[side]), device_id_type=MESH,
        )

    def over_x(side, index):
        ref = piece(side, index, part, False)
        return pltpu.make_async_remote_copy(
            src_ref=ref, dst_ref=ref, send_sem=x_send.at[index], recv_sem=z_recv.at[side, index, 1],
            device_id=partner, device_id_type=MESH,
        )

    def send_before(indices):
        for index in indices:
            over_z(1, index, part).start()

            @pl.when(jnp.logical_not(first))
            def _():
                over_z(1, index, 1 - part).start()

    def send(indices):
        for index in indices:
            over_z(0, index, part).start()

            @pl.when(jnp.logical_not(last))
            def _():
                over_z(0, index, 1 - part).start()

        @pl.when(jnp.logical_not(first))
        def _():
            send_before(indices)

    forwards = (first, last)

    def forward(side, indices):
        @pl.when(forwards[side])
        def _():
            for index in indices:
                over_z(side, index, part).wait_recv()
                over_x(side, index).start()

    def arrive(side, indices):
        for index in indices:
            @pl.when(jnp.logical_not(forwards[side]))
            def _():
                over_z(side, index, part).wait_recv()

            over_z(side, index, 1 - part).wait_recv()

    SLOTS, NEXT, TRIANGLE = (0, 1), (2, 3, 4), (5, 6)
    send(SLOTS)

    for copy in pats:
        copy.wait()

    lane = lax.broadcasted_iota(jnp.int32, (KB, 128), 1)
    slot = lax.broadcasted_iota(jnp.int32, (KB, 128), 0)
    a_of = lane & (W - 1)

    def slot_sum(v):
        for step in (1, 2, 4):
            v = v + pltpu.roll(v, step, 0)
        return v[0:1]

    for q, group in enumerate((before, me, after)):
        off = (pat_v[q] - ((group // TILE) * 128 + lane) + W) & (groups * GROUP - 1)
        for o in range(2 * W + 1):
            code = ((slot ^ (a_of + o)) & 1) * 4 + (slot >> 1) - 8
            tab_v[q, o : o + 1, :] = 8 + slot_sum(jnp.where(off == o, code, 0))
        tab_v[q, 9:10, :] = W * (2 * W + 1) - slot_sum(off)
        if q == 1:
            place = a_of + off
            tab_v[3, 0:KB, :] = ((place ^ slot) & 1) * 6 + (place >> 1)
    table = pltpu.make_async_copy(tab_v, tab_s, tab_sem)
    table.start()
    first_lane = [lax.rem(group, TILE) * GROUP for group in (before, me, after)]

    def swap(v):
        return jnp.concatenate([v[:, BS:], v[:, :BS]], axis=1)

    left_half = lax.broadcasted_iota(jnp.int32, (1, 128), 1) < BS

    def pick(planes, first, second):
        number = jnp.where(left_half, first, second).astype(F32).astype(BF16)
        number = jnp.broadcast_to(number, (BS, 128))
        value = jnp.zeros((BS, 128), BF16)
        for index, plane in planes.items():
            value = jnp.where(number == jnp.array(index, BF16), plane, value)
        return value

    def densify(src, src_base, dst_base, q, first):
        rows = pl.ds(src_base, SB)
        for d in range(4):
            src[rows, 512 + 128 * d : 640 + 128 * d] = swap(src[rows, 128 * d : 128 * d + 128])
        for a in range(W):
            rows = pl.ds(src_base + a * BS, BS)
            planes = {d: src[rows, 128 * d : 128 * d + 128] for d in range(8)}
            for d in range(6):
                number = [
                    tab_s[q, o, first_lane[q] + first + a] if 0 <= o <= 2 * W else 8 for o in (2 * d - a, 2 * d + 1 - a)
                ]
                if all(isinstance(n, int) for n in number):
                    value = jnp.zeros((BS, 128), BF16)
                else:
                    value = pick(planes, *number)
                xd[pl.ds(dst_base + a * BS, BS), 128 * d : 128 * d + 128] = value

    load.wait()
    table.wait()

    def local_rows(index, carry):
        densify(loc, index * SB, (index + 2) * SB, 1, index * W)
        return carry

    lax.fori_loop(0, GROUP // W, local_rows, 0)
    send(NEXT)
    blank = jnp.zeros((128, 128), BF16)
    xd[0:128, 640:768] = blank
    xd[7 * SB + 128 : 8 * SB, 0:128] = blank
    x1[SB + 128 : 2 * SB, 0:128] = blank
    x1[6 * SB : 6 * SB + 128, 640:768] = blank

    block_lane = lax.broadcasted_iota(jnp.int32, (1, SB), 1) >> 6
    eye = jnp.where(
        lax.broadcasted_iota(jnp.int32, (SB, SB), 0) == lax.broadcasted_iota(jnp.int32, (SB, SB), 1), 1.5, 0.0
    ).astype(F32)

    def block(ref, i, j):
        return ref[(i + 2) * SB : (i + 3) * SB, (j - i + 1) * SB : (j - i + 2) * SB]

    def product(left, right, i, j):
        ks = [k for k in (i - 1, i, i + 1) if abs(k - j) <= 1]
        lo = ks[0] - i + 1
        lhs = left[(i + 2) * SB : (i + 3) * SB, lo * SB : (lo + len(ks)) * SB]
        rhs = []
        for k in ks:
            rhs.append(block(right, k, j))
        return jnp.dot(lhs, jnp.concatenate(rhs, axis=0), preferred_element_type=F32)

    def masks(i, j):
        out = []
        for a in range(W):
            r = i * W + a
            q, r = (0, r + GROUP) if r < 0 else ((2, r - GROUP) if r >= GROUP else (1, r))
            o = block_lane + ((j - i + 1) * W - a)
            keep = (o != tab_s[q, 9, first_lane[q] + r]) & (o >= 0) & (o <= 2 * W)
            out.append(jnp.where(keep, 1.0, 0.0).astype(F32))
        return out

    def step(dst, left, right, i, j, factor):
        value = product(left, right, i, j)
        keep = masks(i, j)
        pieces = []
        for a in range(W):
            piece = value[a * BS : (a + 1) * BS]
            if factor:
                piece = piece * (keep[a] * -0.5)
                if i == j:
                    piece = piece + eye[a * BS : (a + 1) * BS]
            else:
                piece = piece * keep[a]
            pieces.append(piece.astype(BF16))
        if dst is x2:
            for a in range(W):
                for h in range(2):
                    d = (j - i + 1) * 2 + h
                    part = pieces[a][:, h * 128 : (h + 1) * 128]
                    rows = slice(i * SB + a * BS, i * SB + (a + 1) * BS)
                    x2[rows, d * 128 : d * 128 + 128] = part
                    x2[rows, (d + 6) * 128 : (d + 6) * 128 + 128] = swap(part)
        else:
            for a in range(W):
                top = (i + 2) * SB + a * BS
                dst[top : top + BS, (j - i + 1) * SB : (j - i + 2) * SB] = pieces[a]

    def level(sides, dst, left, right, pairs, factor):
        for i, j in pairs:
            for side in sides:
                step(dst, left, right, *((i, j) if side == 0 else (3 - i, 3 - j)), factor)

    def level_f0(sides, pairs):
        level(sides, f0, xd, xd, pairs, True)

    def level_x1(sides, pairs):
        level(sides, x1, xd, f0, pairs, False)

    def level_f1(sides, pairs):
        level(sides, f1, x1, x1, pairs, True)

    def level_x2(sides, pairs):
        level(sides, x2, x1, f1, pairs, False)

    outs = []

    def finish(i):
        for a in range(W):
            r = i * W + a
            rows = slice(r * BS, (r + 1) * BS)
            chunks = range(a // 2, a // 2 + W + 1)
            planes = {d: x2[rows, 128 * d : 128 * d + 128] for base in (0, 6) for d in (base + c for c in chunks)}
            for d in range(4):
                number = [tab_s[3, s, first_lane[1] + r] for s in (2 * d, 2 * d + 1)]
                out_v[rows, 128 * d : 128 * d + 128] = pick(planes, *number)
        copy = pltpu.make_async_copy(out_v.at[pl.ds(i * SB, SB)], out_hbm.at[pl.ds(i * SB, SB)], out_sem.at[i])
        copy.start()
        outs.append(copy)

    both = (0, 1)
    level_f0(both, [(0, 1), (1, 0), (1, 1), (1, 2)])
    level_x1(both, [(0, 1), (1, 1), (1, 2)])
    send(TRIANGLE)
    level_f1(both, [(1, 2)])

    def near(side):
        arrive(side, SLOTS)
        densify((a_lo, a_hi)[side], 0, (SB, 6 * SB)[side], (0, 2)[side], (12, 0)[side])
        level_f0((side,), [(0, 0), (0, -1), (-1, 0)])
        level_x1((side,), [(0, 0), (1, 0), (-1, 0)])
        level_f1((side,), [(0, 1), (1, 0), (1, 1)])
        level_x2((side,), [(0, 1), (1, 1)])

    def farther(side):
        arrive(side, NEXT)
        level_f0((side,), [(-1, -1), (-2, -1)])
        level_x1((side,), [(0, -1), (-1, -1), (-2, -1)])
        level_f1((side,), [(0, 0), (0, -1), (-1, 0)])
        level_x2((side,), [(0, 0), (1, 0)])

    def farthest(side):
        arrive(side, TRIANGLE)
        level_f1((side,), [(-1, -1)])
        level_x2((side,), [(0, -1)])

    @pl.when(edge_even)
    def _():
        pl.semaphore_wait(late_x, 1)

    @pl.when(first)
    def _():
        pl.semaphore_wait(late, 1)
        send_before(SLOTS + NEXT + TRIANGLE)

    forward(1, SLOTS)
    near(1)
    forward(1, NEXT)
    forward(0, SLOTS)
    forward(0, NEXT)
    near(0)
    level_x2(both, [(1, 2)])
    forward(1, TRIANGLE)
    forward(0, TRIANGLE)
    farther(1)
    finish(2)
    farther(0)
    finish(1)
    farthest(1)
    finish(3)
    farthest(0)
    finish(0)

    for copy in outs:
        copy.wait()
    for index in SLOTS + NEXT + TRIANGLE:
        over_z(0, index, part).wait_send()
        over_z(1, index, part).wait_send()

        @pl.when(jnp.logical_not(last))
        def _():
            over_z(0, index, 1 - part).wait_send()

        @pl.when(jnp.logical_not(first))
        def _():
            over_z(1, index, 1 - part).wait_send()

        for side in both:
            @pl.when(forwards[side])
            def _():
                over_x(side, index).wait_send()


def solution(mesh):
    groups = mesh.shape["row"] * mesh.shape["col"]
    cols = mesh.shape["col"]

    def on_device(matrix, pattern):
        rows = GROUP * BS

        def body(*refs):
            kernel(groups, cols, *refs)

        any_space = pl.BlockSpec(memory_space=pl.ANY)
        return pl.pallas_call(
            body,
            out_shape=jax.ShapeDtypeStruct((rows, KB * BS), BF16),
            in_specs=[any_space, any_space],
            out_specs=any_space,
            scratch_shapes=[
                pltpu.VMEM((rows, BUF), BF16),
                pltpu.VMEM((SB, BUF), BF16),
                pltpu.VMEM((SB, BUF), BF16),
                pltpu.VMEM((8 * SB, 3 * SB), BF16),
                pltpu.VMEM((8 * SB, 3 * SB), BF16),
                pltpu.VMEM((8 * SB, 3 * SB), BF16),
                pltpu.VMEM((8 * SB, 3 * SB), BF16),
                pltpu.VMEM((rows, 12 * 128), BF16),
                pltpu.VMEM((rows, KB * BS), BF16),
                pltpu.VMEM((3, KB, 128), jnp.int32),
                pltpu.VMEM((4, 16, 128), jnp.int32),
                pltpu.SMEM((4, 16, 128), jnp.int32),
                pltpu.SemaphoreType.DMA,
                pltpu.SemaphoreType.DMA((3,)),
                pltpu.SemaphoreType.DMA,
                pltpu.SemaphoreType.DMA((4,)),
                pltpu.SemaphoreType.DMA((2, 7, 2)),
                pltpu.SemaphoreType.DMA((2, 7, 2)),
                pltpu.SemaphoreType.DMA((7,)),
                pltpu.SemaphoreType.REGULAR,
                pltpu.SemaphoreType.REGULAR,
            ],
            compiler_params=pltpu.CompilerParams(
                collective_id=0, has_side_effects=True, vmem_limit_bytes=62 * 1024 * 1024
            ),
            cost_estimate=pl.CostEstimate(flops=150 * 2 * SB**3, bytes_accessed=8 << 20, transcendentals=0),
        )(matrix, pattern.T)

    return jax.shard_map(
        on_device,
        mesh=mesh,
        in_specs=(P(("row", "col"), None), P()),
        out_specs=P(("row", "col"), None),
        check_vma=False,
    )
```

```python
import jax
import jax.numpy as jnp
from jax import lax
from jax.experimental import pallas as pl
from jax.experimental.pallas import tpu as pltpu
from jax.sharding import PartitionSpec as P

BS = 64
KB = 8
W = 4
SB = W * BS
GROUP = 16
TILE = 128 // GROUP
BUF = 8 * 128
MESH = pl.DeviceIdType.MESH
F32 = jnp.float32
BF16 = jnp.bfloat16


def kernel(
    groups, cols, x_hbm, pat_hbm, out_hbm,
    loc, a_lo, a_hi, xd, f0, x1, f1, x2, out_v,
    pat_v, tab_v, tab_s, load_sem, pat_sem, tab_sem, out_sem, z_send, z_recv, x_send, late, late_x,
):
    row, col, layer = lax.axis_index("row"), lax.axis_index("col"), lax.axis_index("layer")
    me = row * cols + col
    before, after = lax.rem(me + groups - 1, groups), lax.rem(me + 1, groups)

    first, last = col == 0, col == cols - 1
    part = lax.rem(layer, 2)
    partner = (row, col, layer + 1 - 2 * part)

    def device(group):
        return (group // cols, lax.rem(group, cols), layer)

    edge = jnp.logical_or(first, last)
    edge_even, edge_odd = jnp.logical_and(edge, part == 0), jnp.logical_and(edge, part == 1)
    barrier = pltpu.get_barrier_semaphore()
    pl.semaphore_signal(barrier, inc=1, device_id=device(before), device_id_type=MESH)

    @pl.when(edge_even)
    def _():
        pl.semaphore_signal(barrier, inc=1, device_id=partner, device_id_type=MESH)

    @pl.when(jnp.logical_not(last))
    def _():
        pl.semaphore_signal(barrier, inc=1, device_id=device(after), device_id_type=MESH)

    load = pltpu.make_async_copy(x_hbm, loc.at[:, 0 : KB * BS], load_sem)
    load.start()
    def tile_of(group):
        return pl.ds(pl.multiple_of((group // TILE) * 128, 128), 128)

    pats = [
        pltpu.make_async_copy(pat_hbm.at[:, tile_of(group)], pat_v.at[q], pat_sem.at[q])
        for q, group in enumerate((before, me, after))
    ]
    for copy in pats:
        copy.start()
    pl.semaphore_wait(barrier, 2 - jnp.where(first, 1, 0) + jnp.where(edge_odd, 1, 0))

    @pl.when(edge_odd)
    def _():
        pl.semaphore_signal(late_x, inc=1, device_id=partner, device_id_type=MESH)

    @pl.when(last)
    def _():
        pl.semaphore_signal(late, inc=1, device_id=device(after), device_id_type=MESH)

    def piece(side, index, half, source):
        def lanes(base, count, step):
            return pl.ds(pl.multiple_of(base + step * half, 128), count)

        if index < 2:
            rows = pl.ds((3 * SB if source and side == 0 else 0) + 128 * half + 64 * index, 64)
            return x_hbm.at[rows] if source else (a_lo, a_hi)[side].at[rows, 0 : KB * BS]
        if index < 5:
            base = ((4, 3) if source else (0, 7))[side] * SB
            left = (2 * SB, 0)[side]
            if index == 2:
                return xd.at[pl.ds(base + 128 * half, 128), SB : 2 * SB]
            if index == 3:
                return xd.at[pl.ds(base + 128 * half, 128), lanes(left, 128, 128)]
            return xd.at[pl.ds(base + (128, 0)[side] + 64 * half, 64), pl.ds(left + (0, 128)[side], 128)]
        base = ((5, 2) if source else (1, 6))[side] * SB
        left = (0, 2 * SB)[side]
        if index == 5:
            return x1.at[pl.ds(base + 128 * half, 128), lanes(left, 128, 128)]
        return x1.at[pl.ds(base + (0, 128)[side] + 64 * half, 64), pl.ds(left + (128, 0)[side], 128)]

    def over_z(side, index, half):
        mine = jnp.where(half == part, 0, 1)
        return pltpu.make_async_remote_copy(
            src_ref=piece(side, index, half, True), dst_ref=piece(side, index, half, False),
            send_sem=z_send.at[side, index, mine], recv_sem=z_recv.at[side, index, mine],
            device_id=device((after, before)[side]), device_id_type=MESH,
        )

    def over_x(side, index):
        ref = piece(side, index, part, False)
        return pltpu.make_async_remote_copy(
            src_ref=ref, dst_ref=ref, send_sem=x_send.at[index], recv_sem=z_recv.at[side, index, 1],
            device_id=partner, device_id_type=MESH,
        )

    def send_before(indices):
        for index in indices:
            over_z(1, index, part).start()

            @pl.when(jnp.logical_not(first))
            def _():
                over_z(1, index, 1 - part).start()

    def send(indices):
        for index in indices:
            over_z(0, index, part).start()

            @pl.when(jnp.logical_not(last))
            def _():
                over_z(0, index, 1 - part).start()

        @pl.when(jnp.logical_not(first))
        def _():
            send_before(indices)

    forwards = (first, last)

    def forward(side, indices):
        @pl.when(forwards[side])
        def _():
            for index in indices:
                over_z(side, index, part).wait_recv()
                over_x(side, index).start()

    def arrive(side, indices):
        for index in indices:
            @pl.when(jnp.logical_not(forwards[side]))
            def _():
                over_z(side, index, part).wait_recv()

            over_z(side, index, 1 - part).wait_recv()

    SLOTS, NEXT, TRIANGLE = (0, 1), (2, 3, 4), (5, 6)
    send(SLOTS)

    for copy in pats:
        copy.wait()

    lane = lax.broadcasted_iota(jnp.int32, (KB, 128), 1)
    slot = lax.broadcasted_iota(jnp.int32, (KB, 128), 0)
    a_of = lane & (W - 1)

    def slot_sum(v):
        for step in (1, 2, 4):
            v = v + pltpu.roll(v, step, 0)
        return v[0:1]

    for q, group in enumerate((before, me, after)):
        off = (pat_v[q] - ((group // TILE) * 128 + lane) + W) & (groups * GROUP - 1)
        for o in range(2 * W + 1):
            code = ((slot ^ (a_of + o)) & 1) * 4 + (slot >> 1) - 8
            tab_v[q, o : o + 1, :] = 8 + slot_sum(jnp.where(off == o, code, 0))
        tab_v[q, 9:10, :] = W * (2 * W + 1) - slot_sum(off)
        if q == 1:
            place = a_of + off
            tab_v[3, 0:KB, :] = ((place ^ slot) & 1) * 6 + (place >> 1)
    table = pltpu.make_async_copy(tab_v, tab_s, tab_sem)
    table.start()
    first_lane = [lax.rem(group, TILE) * GROUP for group in (before, me, after)]

    def swap(v):
        return jnp.concatenate([v[:, BS:], v[:, :BS]], axis=1)

    left_half = lax.broadcasted_iota(jnp.int32, (1, 128), 1) < BS

    def pick(planes, first, second):
        number = jnp.where(left_half, first, second).astype(F32).astype(BF16)
        number = jnp.broadcast_to(number, (BS, 128))
        value = jnp.zeros((BS, 128), BF16)
        for index, plane in planes.items():
            value = jnp.where(number == jnp.array(index, BF16), plane, value)
        return value

    def densify(src, src_base, dst_base, q, first):
        rows = pl.ds(src_base, SB)
        for d in range(4):
            src[rows, 512 + 128 * d : 640 + 128 * d] = swap(src[rows, 128 * d : 128 * d + 128])
        for a in range(W):
            rows = pl.ds(src_base + a * BS, BS)
            planes = {d: src[rows, 128 * d : 128 * d + 128] for d in range(8)}
            for d in range(6):
                number = [
                    tab_s[q, o, first_lane[q] + first + a] if 0 <= o <= 2 * W else 8 for o in (2 * d - a, 2 * d + 1 - a)
                ]
                if all(isinstance(n, int) for n in number):
                    value = jnp.zeros((BS, 128), BF16)
                else:
                    value = pick(planes, *number)
                xd[pl.ds(dst_base + a * BS, BS), 128 * d : 128 * d + 128] = value

    load.wait()
    table.wait()

    def local_rows(index, carry):
        densify(loc, index * SB, (index + 2) * SB, 1, index * W)
        return carry

    lax.fori_loop(0, GROUP // W, local_rows, 0)
    send(NEXT)
    blank = jnp.zeros((128, 128), BF16)
    xd[0:128, 640:768] = blank
    xd[7 * SB + 128 : 8 * SB, 0:128] = blank
    x1[SB + 128 : 2 * SB, 0:128] = blank
    x1[6 * SB : 6 * SB + 128, 640:768] = blank

    block_lane = lax.broadcasted_iota(jnp.int32, (1, SB), 1) >> 6
    eye = jnp.where(
        lax.broadcasted_iota(jnp.int32, (SB, SB), 0) == lax.broadcasted_iota(jnp.int32, (SB, SB), 1), 1.5, 0.0
    ).astype(F32)

    def block(ref, i, j):
        return ref[(i + 2) * SB : (i + 3) * SB, (j - i + 1) * SB : (j - i + 2) * SB]

    def product(left, right, i, j):
        ks = [k for k in (i - 1, i, i + 1) if abs(k - j) <= 1]
        lo = ks[0] - i + 1
        lhs = left[(i + 2) * SB : (i + 3) * SB, lo * SB : (lo + len(ks)) * SB]
        rhs = []
        for k in ks:
            rhs.append(block(right, k, j))
        return jnp.dot(lhs, jnp.concatenate(rhs, axis=0), preferred_element_type=F32)

    def masks(i, j):
        out = []
        for a in range(W):
            r = i * W + a
            q, r = (0, r + GROUP) if r < 0 else ((2, r - GROUP) if r >= GROUP else (1, r))
            o = block_lane + ((j - i + 1) * W - a)
            keep = (o != tab_s[q, 9, first_lane[q] + r]) & (o >= 0) & (o <= 2 * W)
            out.append(jnp.where(keep, 1.0, 0.0).astype(F32))
        return out

    def step(dst, left, right, i, j, factor):
        value = product(left, right, i, j)
        keep = masks(i, j)
        pieces = []
        for a in range(W):
            piece = value[a * BS : (a + 1) * BS]
            if factor:
                piece = piece * (keep[a] * -0.5)
                if i == j:
                    piece = piece + eye[a * BS : (a + 1) * BS]
            else:
                piece = piece * keep[a]
            pieces.append(piece.astype(BF16))
        if dst is x2:
            for a in range(W):
                for h in range(2):
                    d = (j - i + 1) * 2 + h
                    part = pieces[a][:, h * 128 : (h + 1) * 128]
                    rows = slice(i * SB + a * BS, i * SB + (a + 1) * BS)
                    x2[rows, d * 128 : d * 128 + 128] = part
                    x2[rows, (d + 6) * 128 : (d + 6) * 128 + 128] = swap(part)
        else:
            for a in range(W):
                top = (i + 2) * SB + a * BS
                dst[top : top + BS, (j - i + 1) * SB : (j - i + 2) * SB] = pieces[a]

    def level(sides, dst, left, right, pairs, factor):
        for i, j in pairs:
            for side in sides:
                step(dst, left, right, *((i, j) if side == 0 else (3 - i, 3 - j)), factor)

    def level_f0(sides, pairs):
        level(sides, f0, xd, xd, pairs, True)

    def level_x1(sides, pairs):
        level(sides, x1, xd, f0, pairs, False)

    def level_f1(sides, pairs):
        level(sides, f1, x1, x1, pairs, True)

    def level_x2(sides, pairs):
        level(sides, x2, x1, f1, pairs, False)

    outs = []

    def finish(i):
        for a in range(W):
            r = i * W + a
            rows = slice(r * BS, (r + 1) * BS)
            chunks = range(a // 2, a // 2 + W + 1)
            planes = {d: x2[rows, 128 * d : 128 * d + 128] for base in (0, 6) for d in (base + c for c in chunks)}
            for d in range(4):
                number = [tab_s[3, s, first_lane[1] + r] for s in (2 * d, 2 * d + 1)]
                out_v[rows, 128 * d : 128 * d + 128] = pick(planes, *number)
        copy = pltpu.make_async_copy(out_v.at[pl.ds(i * SB, SB)], out_hbm.at[pl.ds(i * SB, SB)], out_sem.at[i])
        copy.start()
        outs.append(copy)

    both = (0, 1)
    level_f0(both, [(0, 1), (1, 0), (1, 1), (1, 2)])
    level_x1(both, [(0, 1), (1, 1), (1, 2)])
    send(TRIANGLE)
    level_f1(both, [(1, 2)])

    def near(side):
        arrive(side, SLOTS)
        densify((a_lo, a_hi)[side], 0, (SB, 6 * SB)[side], (0, 2)[side], (12, 0)[side])
        level_f0((side,), [(0, 0), (0, -1), (-1, 0)])
        level_x1((side,), [(0, 0), (1, 0), (-1, 0)])
        level_f1((side,), [(0, 1), (1, 0), (1, 1)])
        level_x2((side,), [(0, 1), (1, 1)])

    def farther(side):
        arrive(side, NEXT)
        level_f0((side,), [(-1, -1), (-2, -1)])
        level_x1((side,), [(0, -1), (-1, -1), (-2, -1)])
        level_f1((side,), [(0, 0), (0, -1), (-1, 0)])
        level_x2((side,), [(0, 0), (1, 0)])

    def farthest(side):
        arrive(side, TRIANGLE)
        level_f1((side,), [(-1, -1)])
        level_x2((side,), [(0, -1)])

    @pl.when(edge_even)
    def _():
        pl.semaphore_wait(late_x, 1)

    @pl.when(first)
    def _():
        pl.semaphore_wait(late, 1)
        send_before(SLOTS + NEXT + TRIANGLE)

    forward(1, SLOTS)
    near(1)
    forward(1, NEXT)
    forward(0, SLOTS)

    @pl.when(first)
    def _():
        farther(1)

    forward(0, NEXT)
    near(0)
    forward(1, TRIANGLE)
    forward(0, TRIANGLE)
    level_x2(both, [(1, 2)])

    @pl.when(jnp.logical_not(first))
    def _():
        farther(1)

    finish(2)
    farther(0)
    finish(1)
    farthest(1)
    finish(3)
    farthest(0)
    finish(0)

    for copy in outs:
        copy.wait()
    for index in SLOTS + NEXT + TRIANGLE:
        over_z(0, index, part).wait_send()
        over_z(1, index, part).wait_send()

        @pl.when(jnp.logical_not(last))
        def _():
            over_z(0, index, 1 - part).wait_send()

        @pl.when(jnp.logical_not(first))
        def _():
            over_z(1, index, 1 - part).wait_send()

        for side in both:
            @pl.when(forwards[side])
            def _():
                over_x(side, index).wait_send()


def solution(mesh):
    groups = mesh.shape["row"] * mesh.shape["col"]
    cols = mesh.shape["col"]

    def on_device(matrix, pattern):
        rows = GROUP * BS

        def body(*refs):
            kernel(groups, cols, *refs)

        any_space = pl.BlockSpec(memory_space=pl.ANY)
        return pl.pallas_call(
            body,
            out_shape=pltpu.VMEM((rows, KB * BS), BF16),
            in_specs=[any_space, any_space],
            out_specs=any_space,
            scratch_shapes=[
                pltpu.VMEM((rows, BUF), BF16),
                pltpu.VMEM((SB, BUF), BF16),
                pltpu.VMEM((SB, BUF), BF16),
                pltpu.VMEM((8 * SB, 3 * SB), BF16),
                pltpu.VMEM((8 * SB, 3 * SB), BF16),
                pltpu.VMEM((8 * SB, 3 * SB), BF16),
                pltpu.VMEM((8 * SB, 3 * SB), BF16),
                pltpu.VMEM((rows, 12 * 128), BF16),
                pltpu.VMEM((rows, KB * BS), BF16),
                pltpu.VMEM((3, KB, 128), jnp.int32),
                pltpu.VMEM((4, 16, 128), jnp.int32),
                pltpu.SMEM((4, 16, 128), jnp.int32),
                pltpu.SemaphoreType.DMA,
                pltpu.SemaphoreType.DMA((3,)),
                pltpu.SemaphoreType.DMA,
                pltpu.SemaphoreType.DMA((4,)),
                pltpu.SemaphoreType.DMA((2, 7, 2)),
                pltpu.SemaphoreType.DMA((2, 7, 2)),
                pltpu.SemaphoreType.DMA((7,)),
                pltpu.SemaphoreType.REGULAR,
                pltpu.SemaphoreType.REGULAR,
            ],
            compiler_params=pltpu.CompilerParams(
                collective_id=0, has_side_effects=True, vmem_limit_bytes=56 * 1024 * 1024
            ),
            cost_estimate=pl.CostEstimate(flops=150 * 2 * SB**3, bytes_accessed=8 << 20, transcendentals=0),
        )(matrix, pattern.T)

    return jax.shard_map(
        on_device,
        mesh=mesh,
        in_specs=(P(("row", "col"), None), P()),
        out_specs=P(("row", "col"), None),
        check_vma=False,
    )
```

```python
import jax
import jax.numpy as jnp
from jax import lax
from jax.experimental import pallas as pl
from jax.experimental.pallas import tpu as pltpu
from jax.sharding import PartitionSpec as P

BS = 64
KB = 8
W = 4
SB = W * BS
GROUP = 16
TILE = 128 // GROUP
BUF = 8 * 128
MESH = pl.DeviceIdType.MESH
F32 = jnp.float32
BF16 = jnp.bfloat16


def kernel(
    groups, cols, x_hbm, pat_hbm, out_v,
    loc, a_lo, a_hi, xd, f0, x1, f1, x2,
    pat_v, tab_v, tab_s, load_sem, pat_sem, tab_sem, z_send, z_recv, x_send, late, late_x,
):
    row, col, layer = lax.axis_index("row"), lax.axis_index("col"), lax.axis_index("layer")
    me = row * cols + col
    before, after = lax.rem(me + groups - 1, groups), lax.rem(me + 1, groups)

    first, last = col == 0, col == cols - 1
    part = lax.rem(layer, 2)
    partner = (row, col, layer + 1 - 2 * part)

    def device(group):
        return (group // cols, lax.rem(group, cols), layer)

    edge = jnp.logical_or(first, last)
    edge_even, edge_odd = jnp.logical_and(edge, part == 0), jnp.logical_and(edge, part == 1)
    barrier = pltpu.get_barrier_semaphore()
    pl.semaphore_signal(barrier, inc=1, device_id=device(before), device_id_type=MESH)

    @pl.when(edge_even)
    def _():
        pl.semaphore_signal(barrier, inc=1, device_id=partner, device_id_type=MESH)

    @pl.when(jnp.logical_not(last))
    def _():
        pl.semaphore_signal(barrier, inc=1, device_id=device(after), device_id_type=MESH)

    load = pltpu.make_async_copy(x_hbm, loc.at[:, 0 : KB * BS], load_sem)
    load.start()
    def tile_of(group):
        return pl.ds(pl.multiple_of((group // TILE) * 128, 128), 128)

    pats = [
        pltpu.make_async_copy(pat_hbm.at[:, tile_of(group)], pat_v.at[q], pat_sem.at[q])
        for q, group in enumerate((before, me, after))
    ]
    for copy in pats:
        copy.start()
    pl.semaphore_wait(barrier, 2 - jnp.where(first, 1, 0) + jnp.where(edge_odd, 1, 0))

    @pl.when(edge_odd)
    def _():
        pl.semaphore_signal(late_x, inc=1, device_id=partner, device_id_type=MESH)

    @pl.when(last)
    def _():
        pl.semaphore_signal(late, inc=1, device_id=device(after), device_id_type=MESH)

    def piece(side, index, half, source):
        def lanes(base, count, step):
            return pl.ds(pl.multiple_of(base + step * half, 128), count)

        if index < 2:
            rows = pl.ds((3 * SB if source and side == 0 else 0) + 128 * half + 64 * index, 64)
            return x_hbm.at[rows] if source else (a_lo, a_hi)[side].at[rows, 0 : KB * BS]
        if index < 5:
            base = ((4, 3) if source else (0, 7))[side] * SB
            left = (2 * SB, 0)[side]
            if index == 2:
                return xd.at[pl.ds(base + 128 * half, 128), SB : 2 * SB]
            if index == 3:
                return xd.at[pl.ds(base + 128 * half, 128), lanes(left, 128, 128)]
            return xd.at[pl.ds(base + (128, 0)[side] + 64 * half, 64), pl.ds(left + (0, 128)[side], 128)]
        base = ((5, 2) if source else (1, 6))[side] * SB
        left = (0, 2 * SB)[side]
        if index == 5:
            return x1.at[pl.ds(base + 128 * half, 128), lanes(left, 128, 128)]
        return x1.at[pl.ds(base + (0, 128)[side] + 64 * half, 64), pl.ds(left + (128, 0)[side], 128)]

    def over_z(side, index, half):
        mine = jnp.where(half == part, 0, 1)
        return pltpu.make_async_remote_copy(
            src_ref=piece(side, index, half, True), dst_ref=piece(side, index, half, False),
            send_sem=z_send.at[side, index, mine], recv_sem=z_recv.at[side, index, mine],
            device_id=device((after, before)[side]), device_id_type=MESH,
        )

    def over_x(side, index):
        ref = piece(side, index, part, False)
        return pltpu.make_async_remote_copy(
            src_ref=ref, dst_ref=ref, send_sem=x_send.at[index], recv_sem=z_recv.at[side, index, 1],
            device_id=partner, device_id_type=MESH,
        )

    def send_before(indices):
        for index in indices:
            over_z(1, index, part).start()

            @pl.when(jnp.logical_not(first))
            def _():
                over_z(1, index, 1 - part).start()

    def send(indices):
        for index in indices:
            over_z(0, index, part).start()

            @pl.when(jnp.logical_not(last))
            def _():
                over_z(0, index, 1 - part).start()

        @pl.when(jnp.logical_not(first))
        def _():
            send_before(indices)

    forwards = (first, last)

    def forward(side, indices):
        @pl.when(forwards[side])
        def _():
            for index in indices:
                over_z(side, index, part).wait_recv()
                over_x(side, index).start()

    def arrive(side, indices):
        for index in indices:
            @pl.when(jnp.logical_not(forwards[side]))
            def _():
                over_z(side, index, part).wait_recv()

            over_z(side, index, 1 - part).wait_recv()

    SLOTS, NEXT, TRIANGLE = (0, 1), (2, 3, 4), (5, 6)
    send(SLOTS)

    for copy in pats:
        copy.wait()

    lane = lax.broadcasted_iota(jnp.int32, (KB, 128), 1)
    slot = lax.broadcasted_iota(jnp.int32, (KB, 128), 0)
    a_of = lane & (W - 1)

    def slot_sum(v):
        for step in (1, 2, 4):
            v = v + pltpu.roll(v, step, 0)
        return v[0:1]

    for q, group in enumerate((before, me, after)):
        off = (pat_v[q] - ((group // TILE) * 128 + lane) + W) & (groups * GROUP - 1)
        for o in range(2 * W + 1):
            code = ((slot ^ (a_of + o)) & 1) * 4 + (slot >> 1) - 8
            tab_v[q, o : o + 1, :] = 8 + slot_sum(jnp.where(off == o, code, 0))
        tab_v[q, 9:10, :] = W * (2 * W + 1) - slot_sum(off)
        if q == 1:
            place = a_of + off
            tab_v[3, 0:KB, :] = ((place ^ slot) & 1) * 6 + (place >> 1)
    table = pltpu.make_async_copy(tab_v, tab_s, tab_sem)
    table.start()
    first_lane = [lax.rem(group, TILE) * GROUP for group in (before, me, after)]

    def swap(v):
        return jnp.concatenate([v[:, BS:], v[:, :BS]], axis=1)

    left_half = lax.broadcasted_iota(jnp.int32, (1, 128), 1) < BS

    def pick(planes, first, second):
        number = jnp.where(left_half, first, second).astype(F32).astype(BF16)
        number = jnp.broadcast_to(number, (BS, 128))
        value = jnp.zeros((BS, 128), BF16)
        for index, plane in planes.items():
            value = jnp.where(number == jnp.array(index, BF16), plane, value)
        return value

    def densify(src, src_base, dst_base, q, first):
        rows = pl.ds(src_base, SB)
        for d in range(4):
            src[rows, 512 + 128 * d : 640 + 128 * d] = swap(src[rows, 128 * d : 128 * d + 128])
        for a in range(W):
            rows = pl.ds(src_base + a * BS, BS)
            planes = {d: src[rows, 128 * d : 128 * d + 128] for d in range(8)}
            for d in range(6):
                number = [
                    tab_s[q, o, first_lane[q] + first + a] if 0 <= o <= 2 * W else 8 for o in (2 * d - a, 2 * d + 1 - a)
                ]
                if all(isinstance(n, int) for n in number):
                    value = jnp.zeros((BS, 128), BF16)
                else:
                    value = pick(planes, *number)
                xd[pl.ds(dst_base + a * BS, BS), 128 * d : 128 * d + 128] = value

    load.wait()
    table.wait()

    def local_rows(index, carry):
        densify(loc, index * SB, (index + 2) * SB, 1, index * W)
        return carry

    lax.fori_loop(0, GROUP // W, local_rows, 0)
    send(NEXT)
    blank = jnp.zeros((128, 128), BF16)
    xd[0:128, 640:768] = blank
    xd[7 * SB + 128 : 8 * SB, 0:128] = blank
    x1[SB + 128 : 2 * SB, 0:128] = blank
    x1[6 * SB : 6 * SB + 128, 640:768] = blank

    block_lane = lax.broadcasted_iota(jnp.int32, (1, SB), 1) >> 6
    eye = jnp.where(
        lax.broadcasted_iota(jnp.int32, (SB, SB), 0) == lax.broadcasted_iota(jnp.int32, (SB, SB), 1), 1.5, 0.0
    ).astype(F32)

    def block(ref, i, j):
        return ref[(i + 2) * SB : (i + 3) * SB, (j - i + 1) * SB : (j - i + 2) * SB]

    def product(left, right, i, j):
        ks = [k for k in (i - 1, i, i + 1) if abs(k - j) <= 1]
        lo = ks[0] - i + 1
        lhs = left[(i + 2) * SB : (i + 3) * SB, lo * SB : (lo + len(ks)) * SB]
        rhs = []
        for k in ks:
            rhs.append(block(right, k, j))
        return jnp.dot(lhs, jnp.concatenate(rhs, axis=0), preferred_element_type=F32)

    def masks(i, j):
        out = []
        for a in range(W):
            r = i * W + a
            q, r = (0, r + GROUP) if r < 0 else ((2, r - GROUP) if r >= GROUP else (1, r))
            o = block_lane + ((j - i + 1) * W - a)
            keep = (o != tab_s[q, 9, first_lane[q] + r]) & (o >= 0) & (o <= 2 * W)
            out.append(jnp.where(keep, 1.0, 0.0).astype(F32))
        return out

    def step(dst, left, right, i, j, factor):
        value = product(left, right, i, j)
        keep = masks(i, j)
        pieces = []
        for a in range(W):
            piece = value[a * BS : (a + 1) * BS]
            if factor:
                piece = piece * (keep[a] * -0.5)
                if i == j:
                    piece = piece + eye[a * BS : (a + 1) * BS]
            else:
                piece = piece * keep[a]
            pieces.append(piece.astype(BF16))
        if dst is x2:
            for a in range(W):
                for h in range(2):
                    d = (j - i + 1) * 2 + h
                    part = pieces[a][:, h * 128 : (h + 1) * 128]
                    rows = slice(i * SB + a * BS, i * SB + (a + 1) * BS)
                    x2[rows, d * 128 : d * 128 + 128] = part
                    x2[rows, (d + 6) * 128 : (d + 6) * 128 + 128] = swap(part)
        else:
            for a in range(W):
                top = (i + 2) * SB + a * BS
                dst[top : top + BS, (j - i + 1) * SB : (j - i + 2) * SB] = pieces[a]

    def level(sides, dst, left, right, pairs, factor):
        for i, j in pairs:
            for side in sides:
                step(dst, left, right, *((i, j) if side == 0 else (3 - i, 3 - j)), factor)

    def level_f0(sides, pairs):
        level(sides, f0, xd, xd, pairs, True)

    def level_x1(sides, pairs):
        level(sides, x1, xd, f0, pairs, False)

    def level_f1(sides, pairs):
        level(sides, f1, x1, x1, pairs, True)

    def level_x2(sides, pairs):
        level(sides, x2, x1, f1, pairs, False)

    def finish(i):
        for a in range(W):
            r = i * W + a
            rows = slice(r * BS, (r + 1) * BS)
            chunks = range(a // 2, a // 2 + W + 1)
            planes = {d: x2[rows, 128 * d : 128 * d + 128] for base in (0, 6) for d in (base + c for c in chunks)}
            for d in range(4):
                number = [tab_s[3, s, first_lane[1] + r] for s in (2 * d, 2 * d + 1)]
                out_v[rows, 128 * d : 128 * d + 128] = pick(planes, *number)

    both = (0, 1)
    level_f0(both, [(0, 1), (1, 0), (1, 1), (1, 2)])
    level_x1(both, [(0, 1), (1, 1), (1, 2)])
    send(TRIANGLE)
    level_f1(both, [(1, 2)])

    def near(side):
        arrive(side, SLOTS)
        densify((a_lo, a_hi)[side], 0, (SB, 6 * SB)[side], (0, 2)[side], (12, 0)[side])
        level_f0((side,), [(0, 0), (0, -1), (-1, 0)])
        level_x1((side,), [(0, 0), (1, 0), (-1, 0)])
        level_f1((side,), [(0, 1), (1, 0), (1, 1)])
        level_x2((side,), [(0, 1), (1, 1)])

    def farther(side):
        arrive(side, NEXT)
        level_f0((side,), [(-1, -1), (-2, -1)])
        level_x1((side,), [(0, -1), (-1, -1), (-2, -1)])
        level_f1((side,), [(0, 0), (0, -1), (-1, 0)])
        level_x2((side,), [(0, 0), (1, 0)])

    def farthest(side):
        arrive(side, TRIANGLE)
        level_f1((side,), [(-1, -1)])
        level_x2((side,), [(0, -1)])

    @pl.when(edge_even)
    def _():
        pl.semaphore_wait(late_x, 1)

    @pl.when(first)
    def _():
        pl.semaphore_wait(late, 1)
        send_before(SLOTS + NEXT + TRIANGLE)

    forward(1, SLOTS)
    near(1)
    forward(1, NEXT)
    forward(0, SLOTS)
    forward(0, NEXT)

    @pl.when(first)
    def _():
        farther(1)

    forward(0, TRIANGLE)
    near(0)
    forward(1, TRIANGLE)
    level_x2(both, [(1, 2)])

    @pl.when(jnp.logical_not(first))
    def _():
        farther(1)

    finish(2)
    farthest(1)
    finish(3)
    farther(0)
    farthest(0)
    finish(1)
    finish(0)

    for index in SLOTS + NEXT + TRIANGLE:
        over_z(0, index, part).wait_send()
        over_z(1, index, part).wait_send()

        @pl.when(jnp.logical_not(last))
        def _():
            over_z(0, index, 1 - part).wait_send()

        @pl.when(jnp.logical_not(first))
        def _():
            over_z(1, index, 1 - part).wait_send()

        for side in both:
            @pl.when(forwards[side])
            def _():
                over_x(side, index).wait_send()


def solution(mesh):
    groups = mesh.shape["row"] * mesh.shape["col"]
    cols = mesh.shape["col"]

    def on_device(matrix, pattern):
        rows = GROUP * BS

        def body(*refs):
            kernel(groups, cols, *refs)

        any_space = pl.BlockSpec(memory_space=pl.ANY)
        return pl.pallas_call(
            body,
            out_shape=pltpu.VMEM((rows, KB * BS), BF16),
            in_specs=[any_space, any_space],
            out_specs=pl.BlockSpec(memory_space=pltpu.VMEM),
            scratch_shapes=[
                pltpu.VMEM((rows, BUF), BF16),
                pltpu.VMEM((SB, BUF), BF16),
                pltpu.VMEM((SB, BUF), BF16),
                pltpu.VMEM((8 * SB, 3 * SB), BF16),
                pltpu.VMEM((8 * SB, 3 * SB), BF16),
                pltpu.VMEM((8 * SB, 3 * SB), BF16),
                pltpu.VMEM((8 * SB, 3 * SB), BF16),
                pltpu.VMEM((rows, 12 * 128), BF16),
                pltpu.VMEM((3, KB, 128), jnp.int32),
                pltpu.VMEM((4, 16, 128), jnp.int32),
                pltpu.SMEM((4, 16, 128), jnp.int32),
                pltpu.SemaphoreType.DMA,
                pltpu.SemaphoreType.DMA((3,)),
                pltpu.SemaphoreType.DMA,
                pltpu.SemaphoreType.DMA((2, 7, 2)),
                pltpu.SemaphoreType.DMA((2, 7, 2)),
                pltpu.SemaphoreType.DMA((7,)),
                pltpu.SemaphoreType.REGULAR,
                pltpu.SemaphoreType.REGULAR,
            ],
            compiler_params=pltpu.CompilerParams(
                collective_id=0, has_side_effects=True, vmem_limit_bytes=56 * 1024 * 1024
            ),
            cost_estimate=pl.CostEstimate(flops=150 * 2 * SB**3, bytes_accessed=8 << 20, transcendentals=0),
        )(matrix, pattern.T)

    return jax.shard_map(
        on_device,
        mesh=mesh,
        in_specs=(P(("row", "col"), None), P()),
        out_specs=P(("row", "col"), None),
        check_vma=False,
    )
```
